32 devices in a mesh: groups: 2 (over x), ex: 4 (over y, core), feat: 4 (over z).
Axes of the slice: x: 2, y: 2, z: 4, core: 2. Of those that a mesh axis runs over, the one named last changes fastest.
Arguments:
- layer_input: bfloat16 [1280, 5120], P(('groups', 'ex'), 'feat'), parts along dimension 0, may hold values from -2 to 2
- hidden_grad: bfloat16 [1280, 13824], P(('groups', 'ex'), 'feat'), parts along dimension 0, may hold values from -2 to 2
- hidden_act: bfloat16 [1280, 13824], P(('groups', 'ex'), 'feat'), parts along dimension 0, may hold values from -2 to 2
- output_grad: bfloat16 [1280, 5120], P(('groups', 'ex'), 'feat'), parts along dimension 0, may hold values from -2 to 2
Outputs:
- kernel: float32 [160, 80], P(('groups', 'ex'), 'feat'), parts along dimension 0
The draws below stay inside these ranges and needn't reach their ends.
There are 2 independent parts, one for each index of `groups`. The reference program is written for one: setup_inputs(seed, part) draws one part's arguments, and reference() takes and returns one part's arrays. A program takes and returns all parts, laid end to end along the dimension named above; each array names one. Nothing has to cross between parts.
All inputs are finite; a program needn't handle non-finite values.
Results may differ from the reference program's by a relative error of at most 0.002.
Values may be sent and summed in bfloat16 or wider, within the bound.
No kernel may reach another device: no remote copies, remote signals or barrier semaphores. Data moves between devices by JAX's collectives and lax.ppermute only.
A program may use at most 128 MiB of HBM per device.

```python
import math
import jax
import jax.numpy as jnp

D = 5120
FF = 13824
TOK = 8
EXAMPLES = 80
ROWS = 640


def row_coordinates(key):
    key_centre, key_offset = jax.random.split(jax.random.fold_in(key, 5))
    centres = jax.random.uniform(key_centre, (EXAMPLES, 1), jnp.float32, 0.0, 0.5 * EXAMPLES)
    offsets = jax.random.uniform(key_offset, (EXAMPLES, TOK), jnp.float32, 0.0, 1.5)
    return (centres + offsets).reshape(ROWS, 1)


def panel_law(key, coordinates, width, log_spread):
    key_freq = jax.random.fold_in(key, 0)
    key_phase = jax.random.fold_in(key, 1)
    key_normal = jax.random.fold_in(key, 2)
    key_scale = jax.random.fold_in(key, 4)
    uniform_freq = jax.random.uniform(key_freq, (1, width), jnp.float32, 0.001, 0.999)
    frequency = jnp.clip(jnp.tan(math.pi * (uniform_freq - 0.5)), -40.0, 40.0)
    phases = jax.random.uniform(key_phase, (1, width), jnp.float32, 0.0, 2.0 * math.pi)
    waves = math.sqrt(2.0) * jnp.cos(frequency * coordinates + phases)
    normal_part = jnp.clip(jax.random.normal(key_normal, (ROWS, width), jnp.float32), -5.0, 5.0)
    noise_part = normal_part
    scales = jnp.exp(jax.random.uniform(key_scale, (ROWS, 1), jnp.float32, -log_spread, log_spread))
    values = scales * (waves + noise_part) / math.sqrt(4.0 * width)
    return jnp.clip(values, -2.0, 2.0)


def draw_layer_input(key, part):
    coordinates = row_coordinates(key)
    key = jax.random.fold_in(key, 11)
    return panel_law(key, coordinates, D, math.log(1.4)).astype(jnp.bfloat16)


def draw_hidden_grad(key, part):
    coordinates = row_coordinates(key)
    key = jax.random.fold_in(key, 23)
    return panel_law(key, coordinates, FF, math.log(1.4)).astype(jnp.bfloat16)


def draw_hidden_act(key, part):
    coordinates = row_coordinates(key)
    key = jax.random.fold_in(key, 37)
    return panel_law(key, coordinates, FF, math.log(1.4)).astype(jnp.bfloat16)


def draw_output_grad(key, part):
    coordinates = row_coordinates(key)
    key = jax.random.fold_in(key, 41)
    return panel_law(key, coordinates, D, math.log(1.4)).astype(jnp.bfloat16)


def setup_inputs(seed: int = 0, part: int = 0) -> dict:
    key_list = jax.random.split(jax.random.key(seed), 5)
    part_keys = jax.random.split(jax.random.fold_in(key_list[4], part), 5)
    return {
        "layer_input": draw_layer_input(jax.random.fold_in(jax.random.fold_in(key_list[4], part), 71), part),
        "hidden_grad": draw_hidden_grad(jax.random.fold_in(jax.random.fold_in(key_list[4], part), 71), part),
        "hidden_act": draw_hidden_act(jax.random.fold_in(jax.random.fold_in(key_list[4], part), 71), part),
        "output_grad": draw_output_grad(jax.random.fold_in(jax.random.fold_in(key_list[4], part), 71), part),
    }


def gram(panel):
    return jnp.dot(panel, panel.T, preferred_element_type=jnp.float32)


def reference(layer_input, hidden_grad, hidden_act, output_grad):
    product = gram(layer_input) * gram(hidden_grad) + gram(hidden_act) * gram(output_grad)
    pooled = product.reshape(EXAMPLES, TOK, EXAMPLES, TOK).sum(axis=(1, 3))
    return pooled / jnp.float32(TOK)
```

```python
import functools

import jax
import jax.numpy as jnp
from jax import lax
from jax.experimental import pallas as pl
from jax.experimental.pallas import tpu as pltpu
from jax.sharding import PartitionSpec as P

TOK = 8
SLOT = 32
F32 = jnp.float32
BF16 = jnp.bfloat16


def gram(x, y):
    return lax.dot_general(x, y, (((1,), (1,)), ((), ())), preferred_element_type=F32)


def pool(product, lane):
    rows, cols = product.shape
    by_row = product.reshape(rows // TOK, TOK, cols).sum(axis=1)
    token = lax.broadcasted_iota(jnp.int32, (cols, 128), 0)
    column = lax.broadcasted_iota(jnp.int32, (cols, 128), 1)
    first = (column - lane) * TOK
    spread = jnp.where((token >= first) & (token < first + TOK), 1.0, 0.0).astype(F32)
    return jnp.dot(by_row, spread, precision=lax.Precision.HIGHEST, preferred_element_type=F32)


def narrow_local_kernel(a_in, a_og, b_in, b_og, wide_ref, sent_ref):
    rows = a_in.shape[0]
    wide_ref[0:rows] = gram(a_in[...], a_in[...])
    wide_ref[rows : 2 * rows] = gram(a_og[...], a_og[...])
    core = lax.rem(lax.axis_index("ex"), 2)

    @pl.when(core == 0)
    def _():
        wide_ref[2 * rows : 3 * rows] = gram(a_og[...], b_og[...])

    @pl.when(core == 1)
    def _():
        wide_ref[2 * rows : 3 * rows] = gram(a_in[...], b_in[...])

    sent_ref[...] = wide_ref[...].astype(BF16)


def narrow_cross_kernel(mine, other, wide_ref, sent_ref):
    wide_ref[...] = gram(mine[...], other[...])
    sent_ref[...] = wide_ref[...].astype(BF16)


def wide_local_kernel(a_hg, a_ha, b_hg, b_ha, total, out_ref):
    rows = a_hg.shape[0]
    share = rows // TOK
    diag = gram(a_hg[...], a_hg[...]) * total[0:rows] + gram(a_ha[...], a_ha[...]) * total[rows : 2 * rows]
    out_ref[...] = jnp.zeros_like(out_ref)
    out_ref[0:share] = pool(diag, 0)
    core = lax.rem(lax.axis_index("ex"), 2)

    @pl.when(core == 0)
    def _():
        out_ref[0:share] += pool(gram(a_ha[...], b_ha[...]) * total[2 * rows : 3 * rows], SLOT)

    @pl.when(core == 1)
    def _():
        out_ref[0:share] += pool(gram(a_hg[...], b_hg[...]) * total[2 * rows : 3 * rows], SLOT)


def wide_cross_kernel(mine, other, out_ref):
    out_ref[...] = gram(mine[...], other[...])


def wide_last_kernel(mine, other, before, total, packed, out_ref):
    rows = other.shape[0]
    share = rows // TOK
    product = (before[...] + gram(mine[...], other[...])) * total[...]
    out_ref[...] = packed[...]
    out_ref[0:share] += pool(product[0:rows], 2 * SLOT) + pool(product[rows : 2 * rows], 3 * SLOT)


def final_kernel(blocks, feats, share, mine, sibling, *rest):
    partners, out_ref = rest[:-1], rest[-1]
    me = lax.axis_index("ex")
    z = lax.axis_index("feat")

    def slot(value, index):
        return value[0:share, index * SLOT : index * SLOT + share]

    def turned(value, index):
        return slot(value, index).T

    pieces = [slot(mine, 0), slot(mine, 1) + turned(sibling, 1)]
    for d, partner in enumerate(partners, start=1):
        pieces.append(slot(mine, 2 * d) + turned(partner, 2 * d))
        pieces.append(slot(sibling, 2 * d + 1) + turned(partner, 2 * d + 1))
    per = blocks // feats
    for b in range(per):
        offset = lax.bitwise_xor(z * per + b, me)
        picked = jnp.zeros((share, share), F32)
        for index, piece in enumerate(pieces):
            picked = jnp.where(offset == index, piece, picked)
        out_ref[:, b * share : (b + 1) * share] = picked * F32(1.0 / TOK)


VMEM = pl.BlockSpec(memory_space=pltpu.VMEM)


def call(kernel, n_in, outs, flops, in_specs=None):
    return pl.pallas_call(
        kernel,
        out_shape=outs,
        in_specs=in_specs or [VMEM] * n_in,
        out_specs=jax.tree.map(lambda _: VMEM, outs),
        compiler_params=pltpu.CompilerParams(vmem_limit_bytes=40 * 1024 * 1024),
        cost_estimate=pl.CostEstimate(flops=flops, bytes_accessed=4 * 1024 * 1024, transcendentals=0),
    )


def on_device(blocks, feats, layer_input, hidden_grad, hidden_act, output_grad):
    rows, narrow = layer_input.shape
    wide = hidden_grad.shape[1]
    share = rows // TOK
    chips = blocks // 2
    last = (wide // 128 // 3) * 128
    head = wide - last
    me = lax.axis_index("ex")
    chip = me // 2
    lanes = SLOT * blocks

    def across(value, axis, n, offset):
        return lax.ppermute(value, axis, [(i, i ^ offset) for i in range(n)])

    def sibling(value):
        return across(value, "ex", blocks, 1)

    def sum_feat(value, sent):
        step = 1
        while step < feats:
            got = across(sent, "feat", feats, step)
            value = value + got.astype(F32)
            sent = value.astype(sent.dtype)
            step *= 2
        return value

    def struct(r, c, dtype=F32):
        return jax.ShapeDtypeStruct((r, c), dtype)

    lower = [None] + [(chip & (1 << (d.bit_length() - 1))) == 0 for d in range(1, chips)]

    got_narrow, got_head, got_last = [None], [None], [None]
    for d in range(1, chips):
        got_narrow.append(across(jnp.where(lower[d], layer_input, output_grad), "ex", blocks, 2 * d))
    sends = [None] + [jnp.where(lower[d], hidden_grad, hidden_act) for d in range(1, chips)]
    for d in range(1, chips):
        got_head.append(across(sends[d][:, :head], "ex", blocks, 2 * d))
        got_last.append(across(sends[d][:, head:], "ex", blocks, 2 * d))

    sib_in, sib_og = sibling(layer_input), sibling(output_grad)
    sib_hg, sib_ha = sibling(hidden_grad), sibling(hidden_act)

    local, local_sent = call(
        narrow_local_kernel, 4, (struct(3 * rows, rows), struct(3 * rows, rows, BF16)), 6 * rows * rows * narrow
    )(layer_input, output_grad, sib_in, sib_og)
    local_total = sum_feat(local, local_sent)

    packed = [
        call(wide_local_kernel, 5, struct(24, 128), 6 * rows * rows * wide)(
            hidden_grad, hidden_act, sib_hg, sib_ha, local_total
        )
    ]
    for d in range(1, chips):
        mine_narrow = jnp.concatenate(
            [jnp.where(lower[d], output_grad, layer_input), jnp.where(lower[d], sib_og, sib_in)], axis=0
        )
        mine_wide = jnp.concatenate(
            [jnp.where(lower[d], hidden_act, hidden_grad), jnp.where(lower[d], sib_ha, sib_hg)], axis=0
        )
        cross, cross_sent = call(
            narrow_cross_kernel, 2, (struct(2 * rows, rows), struct(2 * rows, rows, BF16)), 4 * rows * rows * narrow
        )(mine_narrow, got_narrow[d])
        cross_total = sum_feat(cross, cross_sent)
        before = call(wide_cross_kernel, 2, struct(2 * rows, rows), 4 * rows * rows * head)(
            mine_wide[:, :head], got_head[d]
        )
        start = packed[0] if d == 1 else jnp.zeros((24, 128), F32)
        done = call(wide_last_kernel, 5, struct(24, 128), 4 * rows * rows * last)(
            mine_wide[:, head:], got_last[d], before, cross_total, start
        )
        if d == 1:
            packed = [done[:, 0 : 2 * SLOT], done[:, 2 * SLOT :]] if chips > 2 else [done]
        else:
            packed.append(done[:, 2 * SLOT :])
    mine = packed[0] if len(packed) == 1 else jnp.concatenate(packed, axis=1)

    mine = sum_feat(mine, mine)
    others = [across(mine, "ex", blocks, 2 * d) for d in range(1, chips)]
    return call(functools.partial(final_kernel, blocks, feats, share), 2 + len(others), struct(share, share * blocks // feats), 1000)(
        mine, sibling(mine), *others
    )


def solution(mesh):
    spec = P(("groups", "ex"), "feat")
    return jax.shard_map(
        functools.partial(on_device, mesh.shape["ex"], mesh.shape["feat"]),
        mesh=mesh,
        in_specs=(spec, spec, spec, spec),
        out_specs=spec,
        check_vma=False,
    )
```

```python
import functools

import jax
import jax.numpy as jnp
from jax import lax
from jax.experimental import pallas as pl
from jax.experimental.pallas import tpu as pltpu
from jax.sharding import PartitionSpec as P

TOK = 8
SLOT = 32
XL = 1e9
X2 = 1e9
XA = 1e8
F32 = jnp.float32
BF16 = jnp.bfloat16


def gram(x, y):
    return lax.dot_general(x, y, (((1,), (1,)), ((), ())), preferred_element_type=F32)


def pool(product, lane):
    rows, cols = product.shape
    by_row = product.reshape(rows // TOK, TOK, cols).sum(axis=1)
    token = lax.broadcasted_iota(jnp.int32, (cols, 128), 0)
    column = lax.broadcasted_iota(jnp.int32, (cols, 128), 1)
    first = (column - lane) * TOK
    spread = jnp.where((token >= first) & (token < first + TOK), 1.0, 0.0).astype(F32)
    return jnp.dot(by_row, spread, precision=lax.Precision.HIGHEST, preferred_element_type=F32)


def packing(rows, cols):
    whole = cols // 128 * 128
    rest = cols - whole
    parts = 128 // rest if rest and 128 % rest == 0 and rows % (8 * (128 // rest)) == 0 else 1
    return whole, rest, parts


def packed_rows(rows, cols):
    whole, rest, parts = packing(rows, cols)
    return rows * (whole // 128) + (rows // parts if rest else 0)


def pack(ref, at, block):
    rows, cols = block.shape
    whole, rest, parts = packing(rows, cols)
    for tile in range(0, whole, 128):
        ref[at : at + rows, :] = block[:, tile : tile + 128]
        at += rows
    if rest:
        share = rows // parts
        if parts * rest < 128:
            ref[at : at + share, :] = jnp.zeros((share, 128), F32)
        for k in range(parts):
            ref[at : at + share, k * rest : (k + 1) * rest] = block[k * share : (k + 1) * share, whole:]


def unpack(ref, at, rows, cols):
    whole, rest, parts = packing(rows, cols)
    columns = []
    for _ in range(0, whole, 128):
        columns.append(ref[at : at + rows, :])
        at += rows
    if rest:
        share = rows // parts
        columns.append(
            jnp.concatenate([ref[at : at + share, k * rest : (k + 1) * rest] for k in range(parts)], axis=0)
        )
    return columns[0] if len(columns) == 1 else jnp.concatenate(columns, axis=1)


def diagonal_rows(rows):
    return -(-rows // (16 * 128)) * 16


def place(rows):
    return lax.broadcasted_iota(jnp.int32, (rows, rows), 0), lax.broadcasted_iota(jnp.int32, (rows, rows), 1)


def narrow_local_kernel(a_in, a_og, b_in, b_og, total_ref, sent_ref):
    rows = a_in.shape[0]
    size = packed_rows(rows, rows)
    first, second = gram(a_in[...], a_in[...]), gram(a_og[...], a_og[...])
    r, c = place(rows)
    pack(total_ref, 0, jnp.where(r <= c, first, second))
    total_ref[2 * size :] = jnp.zeros((diagonal_rows(rows), 128), F32)
    diagonal = jnp.where(r == c, second, 0.0).sum(axis=0, keepdims=True)
    for k in range(0, rows, 128):
        width = min(128, rows - k)
        total_ref[2 * size + k // 128 : 2 * size + k // 128 + 1, 0:width] = diagonal[:, k : k + width]
    core = lax.rem(lax.axis_index("ex"), 2)

    @pl.when(core == 0)
    def _():
        pack(total_ref, size, gram(a_og[...], b_og[...]))

    @pl.when(core == 1)
    def _():
        pack(total_ref, size, gram(a_in[...], b_in[...]))

    sent_ref[...] = total_ref[...].astype(BF16)


def first_cross_kernel(mine_narrow, got_narrow, mine, got, total_ref, sent_ref, wide_ref):
    rows = got_narrow.shape[0]
    product = gram(mine_narrow[...], got_narrow[...])
    pack(total_ref, 0, product[0:rows])
    pack(total_ref, packed_rows(rows, rows), product[rows : 2 * rows])
    sent_ref[...] = total_ref[...].astype(BF16)
    wide_ref[...] = gram(mine[...], got[...])


def wide_local_kernel(a_hg, a_ha, b_hg, b_ha, total, out_ref):
    rows = a_hg.shape[0]
    size = packed_rows(rows, rows)
    share = rows // TOK
    both = unpack(total, 0, rows, rows)
    second = jnp.concatenate(
        [total[2 * size + k // 128 : 2 * size + k // 128 + 1, 0 : min(128, rows - k)] for k in range(0, rows, 128)], axis=1
    )
    hg, ha = gram(a_hg[...], a_hg[...]), gram(a_ha[...], a_ha[...])
    r, c = place(rows)
    half = jnp.where(r < c, both * hg, jnp.where(r > c, both * ha, 0.5 * (both * hg + second * ha)))
    out_ref[...] = jnp.zeros_like(out_ref)
    out_ref[0:share] = pool(half, 0)
    core = lax.rem(lax.axis_index("ex"), 2)

    @pl.when(core == 0)
    def _():
        out_ref[0:share] += pool(gram(a_ha[...], b_ha[...]) * unpack(total, size, rows, rows), SLOT)

    @pl.when(core == 1)
    def _():
        out_ref[0:share] += pool(gram(a_hg[...], b_hg[...]) * unpack(total, size, rows, rows), SLOT)


def next_cross_kernel(mine, got, before, wide_ref):
    wide_ref[...] = before[...] + gram(mine[...], got[...])


def wide_last_kernel(mine, got, before, total, packed, out_ref):
    rows = got.shape[0]
    share = rows // TOK
    wide = before[...] + gram(mine[...], got[...])
    first = wide[0:rows] * unpack(total, 0, rows, rows)
    second = wide[rows : 2 * rows] * unpack(total, packed_rows(rows, rows), rows, rows)
    out_ref[...] = packed[...]
    out_ref[0:share] += pool(first, 2 * SLOT) + pool(second, 3 * SLOT)


def final_kernel(blocks, feats, share, mine, sibling, *rest):
    partners, out_ref, turned_ref = rest[:-2], rest[-2], rest[-1]
    me = lax.axis_index("ex")
    z = lax.axis_index("feat")
    rows = mine.shape[0]
    lane = lax.broadcasted_iota(jnp.int32, (rows, 128), 1) // SLOT
    straight = []
    for tile in range(blocks // 4):
        cut = slice(tile * 128, (tile + 1) * 128)
        own, sib = mine[:, cut], sibling[:, cut]
        if tile == 0:
            straight.append(jnp.where(lane == 3, sib, own))
            turn = jnp.where(lane == 0, own, jnp.where(lane == 1, sib, partners[0][:, cut]))
        else:
            straight.append(jnp.where(lane % 2 == 1, sib, own))
            turn = jnp.where(lane < 2, partners[2 * tile - 1][:, cut], partners[2 * tile][:, cut])
        turned_ref[cut, 0:rows] = turn.T
    per = blocks // feats
    for b in range(per):
        offset = lax.bitwise_xor(z * per + b, me)
        own = straight[0]
        for tile in range(1, blocks // 4):
            own = jnp.where(offset // 4 == tile, straight[tile], own)
        own = pltpu.roll(own, lax.rem(4 - lax.rem(offset, 4), 4) * SLOT, 1)
        turned = turned_ref[pl.ds(pl.multiple_of(offset * SLOT, SLOT), SLOT), 0:rows]
        out_ref[:, b * share : (b + 1) * share] = (own[0:share, 0:share] + turned[0:share, 0:share]) * F32(1.0 / TOK)


VMEM = pl.BlockSpec(memory_space=pltpu.VMEM)


def call(kernel, n_in, outs, flops, scratch=()):
    return pl.pallas_call(
        kernel,
        out_shape=outs,
        in_specs=[VMEM] * n_in,
        out_specs=jax.tree.map(lambda _: VMEM, outs),
        scratch_shapes=scratch,
        compiler_params=pltpu.CompilerParams(vmem_limit_bytes=40 * 1024 * 1024),
        cost_estimate=pl.CostEstimate(flops=int(flops), bytes_accessed=0, transcendentals=0),
    )


def chunk_bounds(width, hops):
    tiles = width // 128
    step = 0.32 / max(1, hops - 1)
    return [0] + [int(tiles * (0.2 + step * k)) * 128 for k in range(hops)] + [width]


def on_device(blocks, feats, layer_input, hidden_grad, hidden_act, output_grad):
    rows, narrow = layer_input.shape
    wide = hidden_grad.shape[1]
    share = rows // TOK
    share_rows = -(-share // 8) * 8
    chips = blocks // 2
    hops = [1 << k for k in range(feats.bit_length() - 1)]
    cuts = chunk_bounds(wide, len(hops))
    me = lax.axis_index("ex")
    chip = me // 2

    def across(value, axis, n, offset):
        return lax.ppermute(value, axis, [(i, i ^ offset) for i in range(n)])

    def sibling(value):
        return across(value, "ex", blocks, 1)

    def add_feat(value, sent, hop):
        return value + across(sent, "feat", feats, hop).astype(F32)

    def struct(r, c, dtype=F32):
        return jax.ShapeDtypeStruct((r, c), dtype)

    lower = [(chip & (1 << (d.bit_length() - 1))) == 0 for d in range(1, chips)]
    narrow_sends = [jnp.where(low, layer_input, output_grad) for low in lower]
    got_narrow = [across(v, "ex", blocks, 2 * d) for d, v in enumerate(narrow_sends, start=1)]
    sib_in, sib_og = sibling(layer_input), sibling(output_grad)

    size = packed_rows(rows, rows)
    local_rows = 2 * size + diagonal_rows(rows)
    local, sent = call(narrow_local_kernel, 4, (struct(local_rows, 128), struct(local_rows, 128, BF16)), 0)(
        layer_input, output_grad, sib_in, sib_og
    )
    sent, hidden_grad, hidden_act = lax.optimization_barrier((sent, hidden_grad, hidden_act))
    wide_sends = [jnp.where(low, hidden_grad, hidden_act) for low in lower]
    got_wide = [
        [across(v[:, b:e], "ex", blocks, 2 * d) for b, e in zip(cuts[:-1], cuts[1:])]
        for d, v in enumerate(wide_sends, start=1)
    ]
    sib_hg, sib_ha = sibling(hidden_grad), sibling(hidden_act)

    for hop in hops:
        local = add_feat(local, sent, hop)
        sent = local.astype(BF16)
        if hop == 1:
            got_narrow, local, sent = lax.optimization_barrier((got_narrow, local, sent))
    packed = call(wide_local_kernel, 5, struct(share_rows, 128), XL)(hidden_grad, hidden_act, sib_hg, sib_ha, local)

    totals, accs, sents, mines = [], [], [], []
    for d, low in enumerate(lower):
        mine_narrow = jnp.concatenate([jnp.where(low, output_grad, layer_input), jnp.where(low, sib_og, sib_in)], axis=0)
        mine = jnp.concatenate([jnp.where(low, hidden_act, hidden_grad), jnp.where(low, sib_ha, sib_hg)], axis=0)
        total, sent, acc = call(
            first_cross_kernel, 4, (struct(2 * size, 128), struct(2 * size, 128, BF16), struct(2 * rows, rows)), 0
        )(mine_narrow, got_narrow[d], mine[:, : cuts[1]], got_wide[d][0])
        totals.append(total), sents.append(sent), accs.append(acc), mines.append(mine)
    for step, hop in enumerate(hops):
        if step:
            for d in range(chips - 1):
                accs[d] = call(next_cross_kernel, 3, struct(2 * rows, rows), X2)(
                    mines[d][:, cuts[step] : cuts[step + 1]], got_wide[d][step], accs[d]
                )
            if step == len(hops) - 1:
                totals, accs, packed = lax.optimization_barrier((totals, accs, packed))
            else:
                totals, accs = lax.optimization_barrier((totals, accs))
            sents = [t.astype(BF16) for t in totals]
        totals = [add_feat(t, s, hop) for t, s in zip(totals, sents)]

    parts = [packed]
    for d in range(chips - 1):
        start = packed if d == 0 else jnp.zeros((share_rows, 128), F32)
        done = call(wide_last_kernel, 5, struct(share_rows, 128), XA)(
            mines[d][:, cuts[-2] :], got_wide[d][-1], accs[d], totals[d], start
        )
        if d == 0:
            parts = [done]
        else:
            parts.append(done[:, 2 * SLOT :])
    mine = parts[0] if len(parts) == 1 else jnp.concatenate(parts, axis=1)
    for hop in hops:
        mine = add_feat(mine, mine, hop)
    others = [across(mine, "ex", blocks, 2 * d) for d in range(1, chips)]
    return call(
        functools.partial(final_kernel, blocks, feats, share), 1 + blocks // 2, struct(share, share * blocks // feats), 0, [pltpu.VMEM((SLOT * blocks, 128), F32)]
    )(mine, sibling(mine), *others)


def solution(mesh):
    spec = P(("groups", "ex"), "feat")
    return jax.shard_map(
        functools.partial(on_device, mesh.shape["ex"], mesh.shape["feat"]),
        mesh=mesh,
        in_specs=(spec, spec, spec, spec),
        out_specs=spec,
        check_vma=False,
    )
```

```python
import functools

import jax
import jax.numpy as jnp
from jax import lax
from jax.experimental import pallas as pl
from jax.experimental.pallas import tpu as pltpu
from jax.sharding import PartitionSpec as P

TOK = 8
SLOT = 32
XL = 1e9
X2 = 1e9
X3 = 1e7
XA = 1e8
F32 = jnp.float32
BF16 = jnp.bfloat16


def gram(x, y):
    return lax.dot_general(x, y, (((1,), (1,)), ((), ())), preferred_element_type=F32)


def pool(product, lane):
    rows, cols = product.shape
    by_row = product.reshape(rows // TOK, TOK, cols).sum(axis=1)
    token = lax.broadcasted_iota(jnp.int32, (cols, 128), 0)
    column = lax.broadcasted_iota(jnp.int32, (cols, 128), 1)
    first = (column - lane) * TOK
    spread = jnp.where((token >= first) & (token < first + TOK), 1.0, 0.0).astype(BF16)
    high = by_row.astype(BF16)
    low = (by_row - high.astype(F32)).astype(BF16)
    return jnp.dot(high, spread, preferred_element_type=F32) + jnp.dot(low, spread, preferred_element_type=F32)


def packing(rows, cols):
    whole = cols // 128 * 128
    rest = cols - whole
    parts = 128 // rest if rest and 128 % rest == 0 and rows % (8 * (128 // rest)) == 0 else 1
    return whole, rest, parts


def packed_rows(rows, cols):
    whole, rest, parts = packing(rows, cols)
    return rows * (whole // 128) + (rows // parts if rest else 0)


def pack(ref, at, block):
    rows, cols = block.shape
    whole, rest, parts = packing(rows, cols)
    for tile in range(0, whole, 128):
        ref[at : at + rows, :] = block[:, tile : tile + 128]
        at += rows
    if rest:
        share = rows // parts
        if parts * rest < 128:
            ref[at : at + share, :] = jnp.zeros((share, 128), F32)
        for k in range(parts):
            ref[at : at + share, k * rest : (k + 1) * rest] = block[k * share : (k + 1) * share, whole:]


def unpack(ref, at, rows, cols):
    whole, rest, parts = packing(rows, cols)
    columns = []
    for _ in range(0, whole, 128):
        columns.append(ref[at : at + rows, :])
        at += rows
    if rest:
        share = rows // parts
        columns.append(
            jnp.concatenate([ref[at : at + share, k * rest : (k + 1) * rest] for k in range(parts)], axis=0)
        )
    return columns[0] if len(columns) == 1 else jnp.concatenate(columns, axis=1)


def diagonal_rows(rows):
    return -(-rows // (16 * 128)) * 16


def place(rows):
    return lax.broadcasted_iota(jnp.int32, (rows, rows), 0), lax.broadcasted_iota(jnp.int32, (rows, rows), 1)


def narrow_local_kernel(a_in, a_og, b_in, b_og, total_ref, sent_ref):
    rows = a_in.shape[0]
    size = packed_rows(rows, rows)
    first, second = gram(a_in[...], a_in[...]), gram(a_og[...], a_og[...])
    r, c = place(rows)
    pack(total_ref, 0, jnp.where(r <= c, first, second))
    total_ref[2 * size :] = jnp.zeros((diagonal_rows(rows), 128), F32)
    diagonal = jnp.where(r == c, second, 0.0).sum(axis=0, keepdims=True)
    for k in range(0, rows, 128):
        width = min(128, rows - k)
        total_ref[2 * size + k // 128 : 2 * size + k // 128 + 1, 0:width] = diagonal[:, k : k + width]
    core = lax.rem(lax.axis_index("ex"), 2)

    @pl.when(core == 0)
    def _():
        pack(total_ref, size, gram(a_og[...], b_og[...]))

    @pl.when(core == 1)
    def _():
        pack(total_ref, size, gram(a_in[...], b_in[...]))

    sent_ref[...] = total_ref[...].astype(BF16)


def first_cross_kernel(mine_narrow, got_narrow, mine, got, total_ref, sent_ref, wide_ref):
    rows = got_narrow.shape[0]
    product = gram(mine_narrow[...], got_narrow[...])
    pack(total_ref, 0, product[0:rows])
    pack(total_ref, packed_rows(rows, rows), product[rows : 2 * rows])
    sent_ref[...] = total_ref[...].astype(BF16)
    wide_ref[...] = gram(mine[...], got[...])


def wide_local_kernel(a_hg, a_ha, b_hg, b_ha, total, out_ref):
    rows = a_hg.shape[0]
    size = packed_rows(rows, rows)
    share = rows // TOK
    both = unpack(total, 0, rows, rows)
    second = jnp.concatenate(
        [total[2 * size + k // 128 : 2 * size + k // 128 + 1, 0 : min(128, rows - k)] for k in range(0, rows, 128)], axis=1
    )
    hg, ha = gram(a_hg[...], a_hg[...]), gram(a_ha[...], a_ha[...])
    r, c = place(rows)
    half = jnp.where(r < c, both * hg, jnp.where(r > c, both * ha, 0.5 * (both * hg + second * ha)))
    out_ref[...] = jnp.zeros_like(out_ref)
    out_ref[0:share] = pool(half, 0)
    core = lax.rem(lax.axis_index("ex"), 2)

    @pl.when(core == 0)
    def _():
        out_ref[0:share] += pool(gram(a_ha[...], b_ha[...]) * unpack(total, size, rows, rows), SLOT)

    @pl.when(core == 1)
    def _():
        out_ref[0:share] += pool(gram(a_hg[...], b_hg[...]) * unpack(total, size, rows, rows), SLOT)


def next_cross_kernel(mine, got, before, wide_ref):
    wide_ref[...] = before[...] + gram(mine[...], got[...])


def wide_last_kernel(mine, got, before, total, packed, out_ref):
    rows = got.shape[0]
    share = rows // TOK
    wide = before[...] + gram(mine[...], got[...])
    first = wide[0:rows] * unpack(total, 0, rows, rows)
    second = wide[rows : 2 * rows] * unpack(total, packed_rows(rows, rows), rows, rows)
    out_ref[...] = packed[...]
    out_ref[0:share] += pool(first, 2 * SLOT) + pool(second, 3 * SLOT)


def final_kernel(blocks, feats, share, mine, sibling, *rest):
    partners, out_ref, turned_ref = rest[:-2], rest[-2], rest[-1]
    me = lax.axis_index("ex")
    z = lax.axis_index("feat")
    rows = mine.shape[0]
    lane = lax.broadcasted_iota(jnp.int32, (rows, 128), 1) // SLOT
    straight = []
    for tile in range(blocks // 4):
        cut = slice(tile * 128, (tile + 1) * 128)
        own, sib = mine[:, cut], sibling[:, cut]
        if tile == 0:
            straight.append(jnp.where(lane == 3, sib, own))
            turn = jnp.where(lane == 0, own, jnp.where(lane == 1, sib, partners[0][:, cut]))
        else:
            straight.append(jnp.where(lane % 2 == 1, sib, own))
            turn = jnp.where(lane < 2, partners[2 * tile - 1][:, cut], partners[2 * tile][:, cut])
        turned_ref[cut, 0:rows] = turn.T
    per = blocks // feats
    for b in range(per):
        offset = lax.bitwise_xor(z * per + b, me)
        offset = jnp.where(offset >= 2, lax.bitwise_xor(offset, 1), offset)
        own = straight[0]
        for tile in range(1, blocks // 4):
            own = jnp.where(offset // 4 == tile, straight[tile], own)
        own = pltpu.roll(own, lax.rem(4 - lax.rem(offset, 4), 4) * SLOT, 1)
        turned = turned_ref[pl.ds(pl.multiple_of(offset * SLOT, SLOT), SLOT), 0:rows]
        out_ref[:, b * share : (b + 1) * share] = (own[0:share, 0:share] + turned[0:share, 0:share]) * F32(1.0 / TOK)


VMEM = pl.BlockSpec(memory_space=pltpu.VMEM)


def call(kernel, n_in, outs, flops, scratch=()):
    return pl.pallas_call(
        kernel,
        out_shape=outs,
        in_specs=[VMEM] * n_in,
        out_specs=jax.tree.map(lambda _: VMEM, outs),
        scratch_shapes=scratch,
        compiler_params=pltpu.CompilerParams(vmem_limit_bytes=40 * 1024 * 1024),
        cost_estimate=pl.CostEstimate(flops=int(flops), bytes_accessed=0, transcendentals=0),
    )


def chunk_bounds(width, hops):
    tiles = width // 128
    step = 0.32 / max(1, hops - 1)
    return [0] + [int(tiles * (0.2 + step * k)) * 128 for k in range(hops)] + [(tiles - tiles * 4 // 27) * 128, width]


def on_device(blocks, feats, layer_input, hidden_grad, hidden_act, output_grad):
    rows, narrow = layer_input.shape
    wide = hidden_grad.shape[1]
    share = rows // TOK
    share_rows = -(-share // 8) * 8
    chips = blocks // 2
    hops = [1 << k for k in range(feats.bit_length() - 1)]
    cuts = chunk_bounds(wide, len(hops))
    me = lax.axis_index("ex")
    chip = me // 2

    def across(value, axis, n, offset):
        return lax.ppermute(value, axis, [(i, i ^ offset) for i in range(n)])

    def sibling(value):
        return across(value, "ex", blocks, 1)

    def add_feat(value, sent, hop):
        return value + across(sent, "feat", feats, hop).astype(F32)

    def struct(r, c, dtype=F32):
        return jax.ShapeDtypeStruct((r, c), dtype)

    lower = [(chip & (1 << (d.bit_length() - 1))) == 0 for d in range(1, chips)]
    got_narrow = [
        across(jnp.where(low, layer_input, output_grad), "ex", blocks, 2 * d + 1) for d, low in enumerate(lower, start=1)
    ]
    sib_in, sib_og = sibling(layer_input), sibling(output_grad)

    size = packed_rows(rows, rows)
    local_rows = 2 * size + diagonal_rows(rows)
    local, sent = call(narrow_local_kernel, 4, (struct(local_rows, 128), struct(local_rows, 128, BF16)), 0)(
        layer_input, output_grad, sib_in, sib_og
    )
    sent, hidden_grad, hidden_act = lax.optimization_barrier((sent, hidden_grad, hidden_act))
    sends = [jnp.where(low, hidden_grad, hidden_act) for low in lower]
    got_wide = [
        [across(v[:, b:e], "ex", blocks, 2 * d + 1) for b, e in zip(cuts[:-2], cuts[1:-1])] for d, v in enumerate(sends, start=1)
    ]
    sib_hg, sib_ha = sibling(hidden_grad), sibling(hidden_act)

    for hop in hops:
        local = add_feat(local, sent, hop)
        sent = local.astype(BF16)
        if hop == 1:
            sent, sib_hg, sib_ha = lax.optimization_barrier((sent, sib_hg, sib_ha))
            got_narrow, _ = lax.optimization_barrier((got_narrow, local))
    packed = call(wide_local_kernel, 5, struct(share_rows, 128), XL)(hidden_grad, hidden_act, sib_hg, sib_ha, local)

    totals, accs, sents, mines = [], [], [], []
    for d, low in enumerate(lower):
        mine_narrow = jnp.concatenate([jnp.where(low, output_grad, layer_input), jnp.where(low, sib_og, sib_in)], axis=0)
        mine = jnp.concatenate([jnp.where(low, hidden_act, hidden_grad), jnp.where(low, sib_ha, sib_hg)], axis=0)
        total, sent, acc = call(
            first_cross_kernel, 4, (struct(2 * size, 128), struct(2 * size, 128, BF16), struct(2 * rows, rows)), 0
        )(mine_narrow, got_narrow[d], mine[:, : cuts[1]], got_wide[d][0])
        totals.append(total), sents.append(sent), accs.append(acc), mines.append(mine)
    last_sends, accs = lax.optimization_barrier(([v[:, cuts[-2] :] for v in sends], accs))
    for d, v in enumerate(last_sends, start=1):
        got_wide[d - 1].append(across(v, "ex", blocks, 2 * d + 1))
    for step, hop in enumerate(hops):
        if step:
            for d in range(chips - 1):
                accs[d] = call(next_cross_kernel, 3, struct(2 * rows, rows), X2)(
                    mines[d][:, cuts[step] : cuts[step + 1]], got_wide[d][step], accs[d]
                )
            if step == len(hops) - 1:
                totals, accs, packed = lax.optimization_barrier((totals, accs, packed))
            else:
                totals, accs = lax.optimization_barrier((totals, accs))
            sents = [t.astype(BF16) for t in totals]
        totals = [add_feat(t, s, hop) for t, s in zip(totals, sents)]

    parts = [packed]
    for d in range(chips - 1):
        accs[d] = call(next_cross_kernel, 3, struct(2 * rows, rows), X3)(
            mines[d][:, cuts[-3] : cuts[-2]], got_wide[d][-2], accs[d]
        )
        start = packed if d == 0 else jnp.zeros((share_rows, 128), F32)
        done = call(wide_last_kernel, 5, struct(share_rows, 128), XA)(
            mines[d][:, cuts[-2] :], got_wide[d][-1], accs[d], totals[d], start
        )
        if d == 0:
            parts = [done]
        else:
            parts.append(done[:, 2 * SLOT :])
    mine = parts[0] if len(parts) == 1 else jnp.concatenate(parts, axis=1)
    for hop in hops:
        mine = add_feat(mine, mine, hop)
    others = [across(mine, "ex", blocks, 2 * d + 1) for d in range(1, chips)]
    return call(
        functools.partial(final_kernel, blocks, feats, share), 1 + blocks // 2, struct(share, share * blocks // feats), 0, [pltpu.VMEM((SLOT * blocks, 128), F32)]
    )(mine, sibling(mine), *others)


def solution(mesh):
    spec = P(("groups", "ex"), "feat")
    return jax.shard_map(
        functools.partial(on_device, mesh.shape["ex"], mesh.shape["feat"]),
        mesh=mesh,
        in_specs=(spec, spec, spec, spec),
        out_specs=spec,
        check_vma=False,
    )
```

```python
import functools

import jax
import jax.numpy as jnp
from jax import lax
from jax.experimental import pallas as pl
from jax.experimental.pallas import tpu as pltpu
from jax.sharding import PartitionSpec as P

TOK = 8
SLOT = 32
XL = 1e9
X2 = 1e9
X3 = 1e7
XA = 1e8
F32 = jnp.float32
BF16 = jnp.bfloat16


def gram(x, y):
    return lax.dot_general(x, y, (((1,), (1,)), ((), ())), preferred_element_type=F32)


def pool(product, lane):
    rows, cols = product.shape
    by_row = product.reshape(rows // TOK, TOK, cols).sum(axis=1)
    token = lax.broadcasted_iota(jnp.int32, (cols, 128), 0)
    column = lax.broadcasted_iota(jnp.int32, (cols, 128), 1)
    first = (column - lane) * TOK
    spread = jnp.where((token >= first) & (token < first + TOK), 1.0, 0.0).astype(BF16)
    high = by_row.astype(BF16)
    low = (by_row - high.astype(F32)).astype(BF16)
    return jnp.dot(high, spread, preferred_element_type=F32) + jnp.dot(low, spread, preferred_element_type=F32)


def parity(index, size):
    bits = size.bit_length() - 1
    return sum((index // (1 << b)) % 2 for b in range(bits)) % 2


def packing(rows, cols):
    whole = cols // 128 * 128
    rest = cols - whole
    parts = 128 // rest if rest and 128 % rest == 0 and rows % (8 * (128 // rest)) == 0 else 1
    return whole, rest, parts


def packed_rows(rows, cols):
    whole, rest, parts = packing(rows, cols)
    return rows * (whole // 128) + (rows // parts if rest else 0)


def pack(ref, at, block):
    rows, cols = block.shape
    whole, rest, parts = packing(rows, cols)
    for tile in range(0, whole, 128):
        ref[pl.ds(at, rows), :] = block[:, tile : tile + 128]
        at += rows
    if rest:
        share = rows // parts
        if parts * rest < 128:
            ref[pl.ds(at, share), :] = jnp.zeros((share, 128), F32)
        for k in range(parts):
            ref[pl.ds(at, share), k * rest : (k + 1) * rest] = block[k * share : (k + 1) * share, whole:]


def unpack(ref, at, rows, cols):
    whole, rest, parts = packing(rows, cols)
    columns = []
    for _ in range(0, whole, 128):
        columns.append(ref[pl.ds(at, rows), :])
        at += rows
    if rest:
        share = rows // parts
        columns.append(
            jnp.concatenate([ref[pl.ds(at, share), k * rest : (k + 1) * rest] for k in range(parts)], axis=0)
        )
    return columns[0] if len(columns) == 1 else jnp.concatenate(columns, axis=1)


def diagonal_rows(rows):
    return -(-rows // (16 * 128)) * 16


def place(rows):
    return lax.broadcasted_iota(jnp.int32, (rows, rows), 0), lax.broadcasted_iota(jnp.int32, (rows, rows), 1)


def by_role(feats, own, sib, body):
    swapped = parity(lax.axis_index("feat"), feats)
    core = lax.rem(lax.axis_index("ex") + swapped, 2)
    for s, (a, b) in enumerate(((own, sib), (sib, own))):

        @pl.when(swapped == s)
        def _(a=a, b=b):
            body(a, b, core)


def narrow_local_kernel(feats, own_in, own_og, sib_in, sib_og, total_ref, sent_ref):
    rows = own_in.shape[0]
    size = packed_rows(rows, rows)

    def body(a, b, core):
        first, second = gram(a[0][...], a[0][...]), gram(a[1][...], a[1][...])
        r, c = place(rows)
        pack(total_ref, 0, jnp.where(r <= c, first, second))
        total_ref[2 * size :] = jnp.zeros((diagonal_rows(rows), 128), F32)
        diagonal = jnp.where(r == c, second, 0.0).sum(axis=0, keepdims=True)
        for k in range(0, rows, 128):
            width = min(128, rows - k)
            total_ref[2 * size + k // 128 : 2 * size + k // 128 + 1, 0:width] = diagonal[:, k : k + width]

        @pl.when(core == 0)
        def _():
            pack(total_ref, size, gram(a[1][...], b[1][...]))

        @pl.when(core == 1)
        def _():
            pack(total_ref, size, gram(a[0][...], b[0][...]))

    by_role(feats, (own_in, own_og), (sib_in, sib_og), body)
    sent_ref[...] = total_ref[...].astype(BF16)


def role_rows(feats, size):
    swapped = parity(lax.axis_index("feat"), feats)
    return pl.multiple_of(swapped * size, 8), pl.multiple_of((1 - swapped) * size, 8)


def first_cross_kernel(feats, mine_narrow, got_narrow, mine, got, total_ref, sent_ref, wide_ref):
    rows = got_narrow.shape[0]
    product = gram(mine_narrow[...], got_narrow[...])
    for k, at in enumerate(role_rows(feats, packed_rows(rows, rows))):
        pack(total_ref, at, product[k * rows : (k + 1) * rows])
    sent_ref[...] = total_ref[...].astype(BF16)
    wide_ref[...] = gram(mine[...], got[...])


def wide_local_kernel(feats, own_hg, own_ha, sib_hg, sib_ha, total, out_ref):
    rows = own_hg.shape[0]
    size = packed_rows(rows, rows)
    share = rows // TOK
    out_ref[...] = jnp.zeros_like(out_ref)

    def body(a, b, core):
        both = unpack(total, 0, rows, rows)
        second = jnp.concatenate(
            [total[2 * size + k // 128 : 2 * size + k // 128 + 1, 0 : min(128, rows - k)] for k in range(0, rows, 128)],
            axis=1,
        )
        hg, ha = gram(a[0][...], a[0][...]), gram(a[1][...], a[1][...])
        r, c = place(rows)
        half = jnp.where(r < c, both * hg, jnp.where(r > c, both * ha, 0.5 * (both * hg + second * ha)))
        out_ref[0:share] = pool(half, 0)

        @pl.when(core == 0)
        def _():
            out_ref[0:share] += pool(gram(a[1][...], b[1][...]) * unpack(total, size, rows, rows), SLOT)

        @pl.when(core == 1)
        def _():
            out_ref[0:share] += pool(gram(a[0][...], b[0][...]) * unpack(total, size, rows, rows), SLOT)

    by_role(feats, (own_hg, own_ha), (sib_hg, sib_ha), body)


def next_cross_kernel(mine, got, before, wide_ref):
    wide_ref[...] = before[...] + gram(mine[...], got[...])


def wide_last_kernel(feats, mine, got, before, total, packed, out_ref):
    rows = got.shape[0]
    share = rows // TOK
    size = packed_rows(rows, rows)
    wide = before[...] + gram(mine[...], got[...])
    at = role_rows(feats, size)
    first = pool(wide[0:rows] * unpack(total, at[0], rows, rows), 0)
    second = pool(wide[rows : 2 * rows] * unpack(total, at[1], rows, rows), 0)
    swapped = at[0] > 0
    out_ref[...] = packed[...]
    both = jnp.where(swapped, second, first), jnp.where(swapped, first, second)
    out_ref[0:share] += pltpu.roll(both[0], 2 * SLOT, 1) + pltpu.roll(both[1], 3 * SLOT, 1)


def final_kernel(blocks, feats, share, mine, sibling, *rest):
    partners, out_ref, turned_ref = rest[:-2], rest[-2], rest[-1]
    me = lax.axis_index("ex")
    z = lax.axis_index("feat")
    rows = mine.shape[0]
    lane = lax.broadcasted_iota(jnp.int32, (rows, 128), 1) // SLOT
    swapped = parity(z, feats) == 1
    straight = []
    for tile in range(blocks // 4):
        cut = slice(tile * 128, (tile + 1) * 128)
        own = jnp.where(swapped, sibling[:, cut], mine[:, cut])
        sib = jnp.where(swapped, mine[:, cut], sibling[:, cut])
        if tile == 0:
            straight.append(jnp.where(lane == 3, sib, own))
            turn = jnp.where(lane == 0, own, jnp.where(lane == 1, sib, partners[0][:, cut]))
        else:
            straight.append(jnp.where(lane % 2 == 1, sib, own))
            turn = jnp.where(lane < 2, partners[2 * tile - 1][:, cut], partners[2 * tile][:, cut])
        turned_ref[cut, 0:rows] = turn.T
    per = blocks // feats
    for b in range(per):
        offset = lax.bitwise_xor(z * per + b, me)
        offset = jnp.where(offset >= 2, lax.bitwise_xor(offset, 1), offset)
        own = straight[0]
        for tile in range(1, blocks // 4):
            own = jnp.where(offset // 4 == tile, straight[tile], own)
        own = pltpu.roll(own, lax.rem(4 - lax.rem(offset, 4), 4) * SLOT, 1)
        turned = turned_ref[pl.ds(pl.multiple_of(offset * SLOT, SLOT), SLOT), 0:rows]
        out_ref[:, b * share : (b + 1) * share] = (own[0:share, 0:share] + turned[0:share, 0:share]) * F32(1.0 / TOK)


VMEM = pl.BlockSpec(memory_space=pltpu.VMEM)


def call(kernel, n_in, outs, flops, scratch=()):
    return pl.pallas_call(
        kernel,
        out_shape=outs,
        in_specs=[VMEM] * n_in,
        out_specs=jax.tree.map(lambda _: VMEM, outs),
        scratch_shapes=scratch,
        compiler_params=pltpu.CompilerParams(vmem_limit_bytes=40 * 1024 * 1024),
        cost_estimate=pl.CostEstimate(flops=int(flops), bytes_accessed=0, transcendentals=0),
    )


def chunk_bounds(width, hops):
    tiles = width // 128
    step = 0.32 / max(1, hops - 1)
    return [0] + [int(tiles * (0.2 + step * k)) * 128 for k in range(hops)] + [(tiles - tiles * 4 // 27) * 128, width]


def on_device(blocks, feats, layer_input, hidden_grad, hidden_act, output_grad):
    rows, narrow = layer_input.shape
    wide = hidden_grad.shape[1]
    share = rows // TOK
    share_rows = -(-share // 8) * 8
    chips = blocks // 2
    hops = [1 << k for k in range(feats.bit_length() - 1)]
    cuts = chunk_bounds(wide, len(hops))
    me = lax.axis_index("ex")
    chip = me // 2

    def send(value, target):
        pairs = [(e * feats + z, target(e, z)) for e in range(blocks) for z in range(feats)]
        return lax.ppermute(value, ("ex", "feat"), [(i, e * feats + z) for i, (e, z) in pairs])

    def across(value, d):
        return send(value, lambda e, z: (e ^ (2 * d + 1 - parity(z, feats)), z))

    def sibling(value):
        return send(value, lambda e, z: (e ^ 1, z))

    def add_feat(value, sent, hop):
        return value + send(sent, lambda e, z: (e ^ 1, z ^ hop)).astype(F32)

    def struct(r, c, dtype=F32):
        return jax.ShapeDtypeStruct((r, c), dtype)

    lower = [(chip & (1 << (d.bit_length() - 1))) == 0 for d in range(1, chips)]
    picked = [jnp.where(low, layer_input, output_grad) for low in lower]
    picked, layer_input, output_grad, hidden_grad, hidden_act = lax.optimization_barrier(
        (picked, layer_input, output_grad, hidden_grad, hidden_act)
    )
    got_narrow = [across(v, d) for d, v in enumerate(picked, start=1)]
    sib_in, sib_og = sibling(layer_input), sibling(output_grad)

    size = packed_rows(rows, rows)
    local_rows = 2 * size + diagonal_rows(rows)
    local, sent = call(functools.partial(narrow_local_kernel, feats), 4, (struct(local_rows, 128), struct(local_rows, 128, BF16)), 0)(
        layer_input, output_grad, sib_in, sib_og
    )
    sent, hidden_grad, hidden_act = lax.optimization_barrier((sent, hidden_grad, hidden_act))
    sends = [jnp.where(low, hidden_grad, hidden_act) for low in lower]
    got_wide = [
        [across(v[:, b:e], d) for b, e in zip(cuts[:-2], cuts[1:-1])] for d, v in enumerate(sends, start=1)
    ]
    sib_hg, sib_ha = sibling(hidden_grad), sibling(hidden_act)

    for hop in hops:
        local = add_feat(local, sent, hop)
        sent = local.astype(BF16)
        if hop == 1:
            sent, sib_hg, sib_ha = lax.optimization_barrier((sent, sib_hg, sib_ha))
            got_narrow, _ = lax.optimization_barrier((got_narrow, local))
    packed = call(functools.partial(wide_local_kernel, feats), 5, struct(share_rows, 128), XL)(hidden_grad, hidden_act, sib_hg, sib_ha, local)

    totals, accs, sents, mines = [], [], [], []
    for d, low in enumerate(lower):
        mine_narrow = jnp.concatenate([jnp.where(low, output_grad, layer_input), jnp.where(low, sib_og, sib_in)], axis=0)
        mine = jnp.concatenate([jnp.where(low, hidden_act, hidden_grad), jnp.where(low, sib_ha, sib_hg)], axis=0)
        total, sent, acc = call(
            functools.partial(first_cross_kernel, feats), 4, (struct(2 * size, 128), struct(2 * size, 128, BF16), struct(2 * rows, rows)), 0
        )(mine_narrow, got_narrow[d], mine[:, : cuts[1]], got_wide[d][0])
        totals.append(total), sents.append(sent), accs.append(acc), mines.append(mine)
    last_sends, accs = lax.optimization_barrier(([v[:, cuts[-2] :] for v in sends], accs))
    for d, v in enumerate(last_sends, start=1):
        got_wide[d - 1].append(across(v, d))
    for step, hop in enumerate(hops):
        if step:
            for d in range(chips - 1):
                accs[d] = call(next_cross_kernel, 3, struct(2 * rows, rows), X2)(
                    mines[d][:, cuts[step] : cuts[step + 1]], got_wide[d][step], accs[d]
                )
            if step == len(hops) - 1:
                totals, accs, packed = lax.optimization_barrier((totals, accs, packed))
            else:
                totals, accs = lax.optimization_barrier((totals, accs))
            sents = [t.astype(BF16) for t in totals]
        totals = [add_feat(t, s, hop) for t, s in zip(totals, sents)]

    parts = [packed]
    for d in range(chips - 1):
        accs[d] = call(next_cross_kernel, 3, struct(2 * rows, rows), X3)(
            mines[d][:, cuts[-3] : cuts[-2]], got_wide[d][-2], accs[d]
        )
        start = packed if d == 0 else jnp.zeros((share_rows, 128), F32)
        done = call(functools.partial(wide_last_kernel, feats), 5, struct(share_rows, 128), XA)(
            mines[d][:, cuts[-2] :], got_wide[d][-1], accs[d], totals[d], start
        )
        if d == 0:
            parts = [done]
        else:
            parts.append(done[:, 2 * SLOT :])
    mine = parts[0] if len(parts) == 1 else jnp.concatenate(parts, axis=1)
    for hop in hops:
        mine = add_feat(mine, mine, hop)
    others = [across(mine, d) for d in range(1, chips)]
    return call(
        functools.partial(final_kernel, blocks, feats, share), 1 + blocks // 2, struct(share, share * blocks // feats), 0, [pltpu.VMEM((SLOT * blocks, 128), F32)]
    )(mine, sibling(mine), *others)


def solution(mesh):
    spec = P(("groups", "ex"), "feat")
    return jax.shard_map(
        functools.partial(on_device, mesh.shape["ex"], mesh.shape["feat"]),
        mesh=mesh,
        in_specs=(spec, spec, spec, spec),
        out_specs=spec,
        check_vma=False,
    )
```

```python
import functools

import jax
import jax.numpy as jnp
from jax import lax
from jax.experimental import pallas as pl
from jax.experimental.pallas import tpu as pltpu
from jax.sharding import PartitionSpec as P

TOK = 8
SLOT = 32
LOCAL, PIECE, LAST = 1e9, 1e9, 1e8
F32 = jnp.float32
BF16 = jnp.bfloat16


def gram(x, y):
    return lax.dot_general(x, y, (((1,), (1,)), ((), ())), preferred_element_type=F32)


def pool(parts):
    spreads = []
    for product, lane in parts:
        rows, cols = product.shape
        token = lax.broadcasted_iota(jnp.int32, (cols, 128), 0)
        column = lax.broadcasted_iota(jnp.int32, (cols, 128), 1)
        first = (column - lane) * TOK
        spread = jnp.where((token >= first) & (token < first + TOK), 1.0, 0.0).astype(BF16)
        high = product.astype(BF16)
        low = (product - high.astype(F32)).astype(BF16)
        spreads.append(
            jnp.dot(high, spread, preferred_element_type=F32) + jnp.dot(low, spread, preferred_element_type=F32)
        )
    return sum(spreads[1:], spreads[0]).reshape(rows // TOK, TOK, 128).sum(axis=1)


def parity(index, size):
    bits = size.bit_length() - 1
    return sum((index // (1 << b)) % 2 for b in range(bits)) % 2


def packing(rows, cols):
    whole = cols // 128 * 128
    rest = cols - whole
    parts = 128 // rest if rest and 128 % rest == 0 and rows % (8 * (128 // rest)) == 0 else 1
    return whole, rest, parts


def packed_rows(rows, cols):
    whole, rest, parts = packing(rows, cols)
    return rows * (whole // 128) + (rows // parts if rest else 0)


def pack(ref, at, block):
    rows, cols = block.shape
    whole, rest, parts = packing(rows, cols)
    for tile in range(0, whole, 128):
        ref[pl.ds(at, rows), :] = block[:, tile : tile + 128]
        at += rows
    if rest:
        share = rows // parts
        if parts * rest < 128:
            ref[pl.ds(at, share), :] = jnp.zeros((share, 128), F32)
        for k in range(parts):
            ref[pl.ds(at, share), k * rest : (k + 1) * rest] = block[k * share : (k + 1) * share, whole:]


def unpack(ref, at, rows, cols):
    whole, rest, parts = packing(rows, cols)
    columns = []
    for _ in range(0, whole, 128):
        columns.append(ref[pl.ds(at, rows), :])
        at += rows
    if rest:
        share = rows // parts
        columns.append(
            jnp.concatenate([ref[pl.ds(at, share), k * rest : (k + 1) * rest] for k in range(parts)], axis=0)
        )
    return columns[0] if len(columns) == 1 else jnp.concatenate(columns, axis=1)


def diagonal_rows(rows):
    return -(-rows // (16 * 128)) * 16


def place(rows):
    return lax.broadcasted_iota(jnp.int32, (rows, rows), 0), lax.broadcasted_iota(jnp.int32, (rows, rows), 1)


def by_role(feats, own, sib, body):
    swapped = parity(lax.axis_index("feat"), feats)
    core = lax.rem(lax.axis_index("ex") + swapped, 2)
    for s, (a, b) in enumerate(((own, sib), (sib, own))):

        @pl.when(swapped == s)
        def _(a=a, b=b):
            body(a, b, core)


def narrow_local_kernel(feats, own_in, own_og, sib_in, sib_og, total_ref, sent_ref):
    rows = own_in.shape[0]
    size = packed_rows(rows, rows)

    def body(a, b, core):
        first, second = gram(a[0][...], a[0][...]), gram(a[1][...], a[1][...])
        r, c = place(rows)
        pack(total_ref, 0, jnp.where(r <= c, first, second))
        total_ref[2 * size :] = jnp.zeros((diagonal_rows(rows), 128), F32)
        diagonal = jnp.where(r == c, second, 0.0).sum(axis=0, keepdims=True)
        for k in range(0, rows, 128):
            width = min(128, rows - k)
            total_ref[2 * size + k // 128 : 2 * size + k // 128 + 1, 0:width] = diagonal[:, k : k + width]

        @pl.when(core == 0)
        def _():
            pack(total_ref, size, gram(a[1][...], b[1][...]))

        @pl.when(core == 1)
        def _():
            pack(total_ref, size, gram(a[0][...], b[0][...]))

    by_role(feats, (own_in, own_og), (sib_in, sib_og), body)
    sent_ref[...] = total_ref[...].astype(BF16)


def role_rows(feats, size):
    swapped = parity(lax.axis_index("feat"), feats)
    return pl.multiple_of(swapped * size, 8), pl.multiple_of((1 - swapped) * size, 8)


def first_cross_kernel(feats, mine_narrow, got_narrow, mine, got, total_ref, sent_ref, wide_ref):
    rows = got_narrow.shape[0]
    product = gram(mine_narrow[...], got_narrow[...])
    for k, at in enumerate(role_rows(feats, packed_rows(rows, rows))):
        pack(total_ref, at, product[k * rows : (k + 1) * rows])
    sent_ref[...] = total_ref[...].astype(BF16)
    wide_ref[...] = gram(mine[...], got[...])


def wide_local_kernel(feats, own_hg, own_ha, sib_hg, sib_ha, total, out_ref):
    rows = own_hg.shape[0]
    size = packed_rows(rows, rows)
    share = rows // TOK
    out_ref[...] = jnp.zeros_like(out_ref)

    def body(a, b, core):
        both = unpack(total, 0, rows, rows)
        second = jnp.concatenate(
            [total[2 * size + k // 128 : 2 * size + k // 128 + 1, 0 : min(128, rows - k)] for k in range(0, rows, 128)],
            axis=1,
        )
        hg, ha = gram(a[0][...], a[0][...]), gram(a[1][...], a[1][...])
        r, c = place(rows)
        half = jnp.where(r < c, both * hg, jnp.where(r > c, both * ha, 0.5 * (both * hg + second * ha)))
        out_ref[0:share] = pool([(half, 0)])

        @pl.when(core == 0)
        def _():
            out_ref[0:share] += pool([(gram(a[1][...], b[1][...]) * unpack(total, size, rows, rows), SLOT)])

        @pl.when(core == 1)
        def _():
            out_ref[0:share] += pool([(gram(a[0][...], b[0][...]) * unpack(total, size, rows, rows), SLOT)])

    by_role(feats, (own_hg, own_ha), (sib_hg, sib_ha), body)


def next_cross_kernel(mine, got, before, wide_ref):
    wide_ref[...] = before[...] + gram(mine[...], got[...])


def wide_last_kernel(feats, mine, got, before, total, packed, out_ref):
    rows = got.shape[0]
    share = rows // TOK
    size = packed_rows(rows, rows)
    wide = before[...] + gram(mine[...], got[...])
    at = role_rows(feats, size)
    swapped = parity(lax.axis_index("feat"), feats)
    first = wide[0:rows] * unpack(total, at[0], rows, rows)
    second = wide[rows : 2 * rows] * unpack(total, at[1], rows, rows)
    out_ref[...] = packed[...]
    out_ref[0:share] += pool([(first, (2 + swapped) * SLOT), (second, (3 - swapped) * SLOT)])


def final_kernel(blocks, feats, share, mine, sibling, *rest):
    partners, out_ref, turned_ref = rest[:-2], rest[-2], rest[-1]
    me = lax.axis_index("ex")
    z = lax.axis_index("feat")
    rows = mine.shape[0]
    lane = lax.broadcasted_iota(jnp.int32, (rows, 128), 1) // SLOT
    swapped = parity(z, feats) == 1
    straight = []
    for tile in range(blocks // 4):
        cut = slice(tile * 128, (tile + 1) * 128)
        own = jnp.where(swapped, sibling[:, cut], mine[:, cut])
        sib = jnp.where(swapped, mine[:, cut], sibling[:, cut])
        if tile == 0:
            straight.append(jnp.where(lane == 3, sib, own))
            turn = jnp.where(lane == 0, own, jnp.where(lane == 1, sib, partners[0][:, cut]))
        else:
            straight.append(jnp.where(lane % 2 == 1, sib, own))
            turn = jnp.where(lane < 2, partners[2 * tile - 1][:, cut], partners[2 * tile][:, cut])
        turned_ref[cut, 0:rows] = turn.T
    per = blocks // feats
    for b in range(per):
        offset = lax.bitwise_xor(z * per + b, me)
        offset = jnp.where(offset >= 2, lax.bitwise_xor(offset, 1), offset)
        own = straight[0]
        for tile in range(1, blocks // 4):
            own = jnp.where(offset // 4 == tile, straight[tile], own)
        own = pltpu.roll(own, lax.rem(4 - lax.rem(offset, 4), 4) * SLOT, 1)
        turned = turned_ref[pl.ds(pl.multiple_of(offset * SLOT, SLOT), SLOT), 0:rows]
        out_ref[:, b * share : (b + 1) * share] = (own[0:share, 0:share] + turned[0:share, 0:share]) * F32(1.0 / TOK)


VMEM = pl.BlockSpec(memory_space=pltpu.VMEM)


def call(kernel, n_in, outs, flops, scratch=()):
    return pl.pallas_call(
        kernel,
        out_shape=outs,
        in_specs=[VMEM] * n_in,
        out_specs=jax.tree.map(lambda _: VMEM, outs),
        scratch_shapes=scratch,
        compiler_params=pltpu.CompilerParams(vmem_limit_bytes=40 * 1024 * 1024),
        cost_estimate=pl.CostEstimate(flops=int(flops), bytes_accessed=0, transcendentals=0),
    )


def chunk_bounds(width, hops):
    tiles = width // 128
    step = 0.25 / max(1, hops - 1)
    return [0] + [int(tiles * (0.2 + step * k)) * 128 for k in range(hops)] + [(tiles - max(1, tiles * 4 // 27)) * 128, width]


def on_device(blocks, feats, layer_input, hidden_grad, hidden_act, output_grad):
    rows, narrow = layer_input.shape
    wide = hidden_grad.shape[1]
    share = rows // TOK
    share_rows = -(-share // 8) * 8
    chips = blocks // 2
    hops = [1 << k for k in range(feats.bit_length() - 1)]
    cuts = chunk_bounds(wide, len(hops))
    me = lax.axis_index("ex")
    chip = me // 2

    def send(value, target):
        pairs = [(e * feats + z, target(e, z)) for e in range(blocks) for z in range(feats)]
        return lax.ppermute(value, ("ex", "feat"), [(i, e * feats + z) for i, (e, z) in pairs])

    def across(value, d):
        return send(value, lambda e, z: (e ^ (2 * d + 1 - parity(z, feats)), z))

    def sibling(value):
        return send(value, lambda e, z: (e ^ 1, z))

    def add_feat(value, sent, hop):
        return value + send(sent, lambda e, z: (e ^ 1, z ^ hop)).astype(F32)

    def struct(r, c, dtype=F32):
        return jax.ShapeDtypeStruct((r, c), dtype)

    lower = [(chip & (1 << (d.bit_length() - 1))) == 0 for d in range(1, chips)]
    picked = [jnp.where(low, layer_input, output_grad) for low in lower]
    picked, layer_input, output_grad, hidden_grad, hidden_act = lax.optimization_barrier(
        (picked, layer_input, output_grad, hidden_grad, hidden_act)
    )
    got_narrow = [across(v, d) for d, v in enumerate(picked, start=1)]
    sib_in, sib_og = sibling(layer_input), sibling(output_grad)

    size = packed_rows(rows, rows)
    local_rows = 2 * size + diagonal_rows(rows)
    local, sent = call(functools.partial(narrow_local_kernel, feats), 4, (struct(local_rows, 128), struct(local_rows, 128, BF16)), 0)(
        layer_input, output_grad, sib_in, sib_og
    )
    sent, hidden_grad, hidden_act = lax.optimization_barrier((sent, hidden_grad, hidden_act))
    sends = [jnp.where(low, hidden_grad, hidden_act) for low in lower]
    got_wide = [
        [across(v[:, b:e], d) for b, e in zip(cuts[:-2], cuts[1:-1])] for d, v in enumerate(sends, start=1)
    ]
    sib_hg, sib_ha = sibling(hidden_grad), sibling(hidden_act)

    for hop in hops:
        local = add_feat(local, sent, hop)
        sent = local.astype(BF16)
        if hop == 1:
            sent, sib_hg, sib_ha = lax.optimization_barrier((sent, sib_hg, sib_ha))
            got_narrow, _ = lax.optimization_barrier((got_narrow, local))
    totals, accs, sents, mines = [], [], [], []
    for d, low in enumerate(lower):
        mine_narrow = jnp.concatenate([jnp.where(low, output_grad, layer_input), jnp.where(low, sib_og, sib_in)], axis=0)
        mine = jnp.concatenate([jnp.where(low, hidden_act, hidden_grad), jnp.where(low, sib_ha, sib_hg)], axis=0)
        total, sent, acc = call(
            functools.partial(first_cross_kernel, feats), 4, (struct(2 * size, 128), struct(2 * size, 128, BF16), struct(2 * rows, rows)), 0
        )(mine_narrow, got_narrow[d], mine[:, : cuts[1]], got_wide[d][0])
        totals.append(total), sents.append(sent), accs.append(acc), mines.append(mine)
    last_sends, accs = lax.optimization_barrier(([v[:, cuts[-2] :] for v in sends], accs))
    for d, v in enumerate(last_sends, start=1):
        got_wide[d - 1].append(across(v, d))
    for step, hop in enumerate(hops):
        if step:
            for d in range(chips - 1):
                accs[d] = call(next_cross_kernel, 3, struct(2 * rows, rows), PIECE)(
                    mines[d][:, cuts[step] : cuts[step + 1]], got_wide[d][step], accs[d]
                )
            if step == len(hops) - 1:
                totals, accs, local = lax.optimization_barrier((totals, accs, local))
            else:
                totals, accs = lax.optimization_barrier((totals, accs))
            sents = [t.astype(BF16) for t in totals]
        totals = [add_feat(t, s, hop) for t, s in zip(totals, sents)]

    packed = call(functools.partial(wide_local_kernel, feats), 5, struct(share_rows, 128), LOCAL)(hidden_grad, hidden_act, sib_hg, sib_ha, local)
    parts = [packed]
    for d in range(chips - 1):
        accs[d] = call(next_cross_kernel, 3, struct(2 * rows, rows), LAST)(
            mines[d][:, cuts[-3] : cuts[-2]], got_wide[d][-2], accs[d]
        )
        start = packed if d == 0 else jnp.zeros((share_rows, 128), F32)
        done = call(functools.partial(wide_last_kernel, feats), 5, struct(share_rows, 128), LAST)(
            mines[d][:, cuts[-2] :], got_wide[d][-1], accs[d], totals[d], start
        )
        if d == 0:
            parts = [done]
        else:
            parts.append(done[:, 2 * SLOT :])
    mine = parts[0] if len(parts) == 1 else jnp.concatenate(parts, axis=1)
    for hop in hops:
        mine = add_feat(mine, mine, hop)
    others = [across(mine, d) for d in range(1, chips)]
    return call(
        functools.partial(final_kernel, blocks, feats, share), 1 + blocks // 2, struct(share, share * blocks // feats), 0, [pltpu.VMEM((SLOT * blocks, 128), F32)]
    )(mine, sibling(mine), *others)


def solution(mesh):
    spec = P(("groups", "ex"), "feat")
    return jax.shard_map(
        functools.partial(on_device, mesh.shape["ex"], mesh.shape["feat"]),
        mesh=mesh,
        in_specs=(spec, spec, spec, spec),
        out_specs=spec,
        check_vma=False,
    )
```

```python
import functools

import jax
import jax.numpy as jnp
from jax import lax
from jax.experimental import pallas as pl
from jax.experimental.pallas import tpu as pltpu
from jax.sharding import PartitionSpec as P

TOK = 8
SLOT = 32
LOCAL, PIECE, LAST = 1e9, 1e9, 1e8
F32 = jnp.float32
BF16 = jnp.bfloat16


def gram(x, y):
    return lax.dot_general(x, y, (((1,), (1,)), ((), ())), preferred_element_type=F32)


def pool(parts):
    spreads = []
    for product, lane in parts:
        rows, cols = product.shape
        token = lax.broadcasted_iota(jnp.int32, (cols, 128), 0)
        column = lax.broadcasted_iota(jnp.int32, (cols, 128), 1)
        first = (column - lane) * TOK
        spread = jnp.where((token >= first) & (token < first + TOK), 1.0, 0.0).astype(BF16)
        high = product.astype(BF16)
        low = (product - high.astype(F32)).astype(BF16)
        spreads.append(
            jnp.dot(high, spread, preferred_element_type=F32) + jnp.dot(low, spread, preferred_element_type=F32)
        )
    return sum(spreads[1:], spreads[0]).reshape(rows // TOK, TOK, 128).sum(axis=1)


def parity(index, size):
    bits = size.bit_length() - 1
    return sum((index // (1 << b)) % 2 for b in range(bits)) % 2


def packing(rows, cols):
    whole = cols // 128 * 128
    rest = cols - whole
    parts = 128 // rest if rest and 128 % rest == 0 and rows % (8 * (128 // rest)) == 0 else 1
    return whole, rest, parts


def packed_rows(rows, cols):
    whole, rest, parts = packing(rows, cols)
    return rows * (whole // 128) + (rows // parts if rest else 0)


def pack(ref, at, block):
    rows, cols = block.shape
    whole, rest, parts = packing(rows, cols)
    for tile in range(0, whole, 128):
        ref[pl.ds(at, rows), :] = block[:, tile : tile + 128]
        at += rows
    if rest:
        share = rows // parts
        if parts * rest < 128:
            ref[pl.ds(at, share), :] = jnp.zeros((share, 128), F32)
        for k in range(parts):
            ref[pl.ds(at, share), k * rest : (k + 1) * rest] = block[k * share : (k + 1) * share, whole:]


def unpack(ref, at, rows, cols):
    whole, rest, parts = packing(rows, cols)
    columns = []
    for _ in range(0, whole, 128):
        columns.append(ref[pl.ds(at, rows), :])
        at += rows
    if rest:
        share = rows // parts
        columns.append(
            jnp.concatenate([ref[pl.ds(at, share), k * rest : (k + 1) * rest] for k in range(parts)], axis=0)
        )
    return columns[0] if len(columns) == 1 else jnp.concatenate(columns, axis=1)


def diagonal_rows(rows):
    return -(-rows // (16 * 128)) * 16


def place(rows):
    return lax.broadcasted_iota(jnp.int32, (rows, rows), 0), lax.broadcasted_iota(jnp.int32, (rows, rows), 1)


def by_role(feats, own, sib, body):
    swapped = parity(lax.axis_index("feat"), feats)
    core = lax.rem(lax.axis_index("ex") + swapped, 2)
    for s, (a, b) in enumerate(((own, sib), (sib, own))):

        @pl.when(swapped == s)
        def _(a=a, b=b):
            body(a, b, core)


def narrow_local_kernel(feats, own_in, own_og, sib_in, sib_og, total_ref, sent_ref):
    rows = own_in.shape[0]
    size = packed_rows(rows, rows)

    def body(a, b, core):
        first, second = gram(a[0][...], a[0][...]), gram(a[1][...], a[1][...])
        r, c = place(rows)
        pack(total_ref, 0, jnp.where(r <= c, first, second))
        total_ref[2 * size :] = jnp.zeros((diagonal_rows(rows), 128), F32)
        diagonal = jnp.where(r == c, second, 0.0).sum(axis=0, keepdims=True)
        for k in range(0, rows, 128):
            width = min(128, rows - k)
            total_ref[2 * size + k // 128 : 2 * size + k // 128 + 1, 0:width] = diagonal[:, k : k + width]

        @pl.when(core == 0)
        def _():
            pack(total_ref, size, gram(a[1][...], b[1][...]))

        @pl.when(core == 1)
        def _():
            pack(total_ref, size, gram(a[0][...], b[0][...]))

    by_role(feats, (own_in, own_og), (sib_in, sib_og), body)
    sent_ref[...] = total_ref[...].astype(BF16)


def role_rows(feats, size):
    swapped = parity(lax.axis_index("feat"), feats)
    return pl.multiple_of(swapped * size, 8), pl.multiple_of((1 - swapped) * size, 8)


def first_cross_kernel(feats, mine_narrow, got_narrow, mine, got, total_ref, sent_ref, wide_ref):
    rows = got_narrow.shape[0]
    product = gram(mine_narrow[...], got_narrow[...])
    for k, at in enumerate(role_rows(feats, packed_rows(rows, rows))):
        pack(total_ref, at, product[k * rows : (k + 1) * rows])
    sent_ref[...] = total_ref[...].astype(BF16)
    wide_ref[...] = gram(mine[...], got[...])


def wide_local_kernel(feats, own_hg, own_ha, sib_hg, sib_ha, total, out_ref):
    rows = own_hg.shape[0]
    size = packed_rows(rows, rows)
    share = rows // TOK
    out_ref[...] = jnp.zeros_like(out_ref)

    def body(a, b, core):
        both = unpack(total, 0, rows, rows)
        second = jnp.concatenate(
            [total[2 * size + k // 128 : 2 * size + k // 128 + 1, 0 : min(128, rows - k)] for k in range(0, rows, 128)],
            axis=1,
        )
        hg, ha = gram(a[0][...], a[0][...]), gram(a[1][...], a[1][...])
        r, c = place(rows)
        half = jnp.where(r < c, both * hg, jnp.where(r > c, both * ha, 0.5 * (both * hg + second * ha)))
        out_ref[0:share] = pool([(half, 0)])

        @pl.when(core == 0)
        def _():
            out_ref[0:share] += pool([(gram(a[1][...], b[1][...]) * unpack(total, size, rows, rows), SLOT)])

        @pl.when(core == 1)
        def _():
            out_ref[0:share] += pool([(gram(a[0][...], b[0][...]) * unpack(total, size, rows, rows), SLOT)])

    by_role(feats, (own_hg, own_ha), (sib_hg, sib_ha), body)


def next_cross_kernel(mine, got, before, wide_ref):
    wide_ref[...] = before[...] + gram(mine[...], got[...])


def wide_last_kernel(feats, mine, got, before, total, packed, out_ref):
    rows = got.shape[0]
    share = rows // TOK
    size = packed_rows(rows, rows)
    wide = before[...] + gram(mine[...], got[...])
    at = role_rows(feats, size)
    swapped = parity(lax.axis_index("feat"), feats)
    first = wide[0:rows] * unpack(total, at[0], rows, rows)
    second = wide[rows : 2 * rows] * unpack(total, at[1], rows, rows)
    out_ref[...] = packed[...]
    out_ref[0:share] += pool([(first, (2 + swapped) * SLOT), (second, (3 - swapped) * SLOT)])


def final_kernel(blocks, feats, share, mine, sibling, *rest):
    partners, out_ref, turned_ref = rest[:-2], rest[-2], rest[-1]
    me = lax.axis_index("ex")
    z = lax.axis_index("feat")
    rows = mine.shape[0]
    lane = lax.broadcasted_iota(jnp.int32, (rows, 128), 1) // SLOT
    swapped = parity(z, feats) == 1
    straight = []
    for tile in range(blocks // 4):
        cut = slice(tile * 128, (tile + 1) * 128)
        own = jnp.where(swapped, sibling[:, cut], mine[:, cut])
        sib = jnp.where(swapped, mine[:, cut], sibling[:, cut])
        if tile == 0:
            straight.append(jnp.where(lane == 3, sib, own))
            turn = jnp.where(lane == 0, own, jnp.where(lane == 1, sib, partners[0][:, cut]))
        else:
            straight.append(jnp.where(lane % 2 == 1, sib, own))
            turn = jnp.where(lane < 2, partners[2 * tile - 1][:, cut], partners[2 * tile][:, cut])
        turned_ref[cut, 0:rows] = turn.T
    per = blocks // feats
    for b in range(per):
        offset = lax.bitwise_xor(z * per + b, me)
        offset = jnp.where(offset >= 2, lax.bitwise_xor(offset, 1), offset)
        own = straight[0]
        for tile in range(1, blocks // 4):
            own = jnp.where(offset // 4 == tile, straight[tile], own)
        own = pltpu.roll(own, lax.rem(4 - lax.rem(offset, 4), 4) * SLOT, 1)
        turned = turned_ref[pl.ds(pl.multiple_of(offset * SLOT, SLOT), SLOT), 0:rows]
        out_ref[:, b * share : (b + 1) * share] = (own[0:share, 0:share] + turned[0:share, 0:share]) * F32(1.0 / TOK)


VMEM = pl.BlockSpec(memory_space=pltpu.VMEM)


def call(kernel, n_in, outs, flops, scratch=()):
    return pl.pallas_call(
        kernel,
        out_shape=outs,
        in_specs=[VMEM] * n_in,
        out_specs=jax.tree.map(lambda _: VMEM, outs),
        scratch_shapes=scratch,
        compiler_params=pltpu.CompilerParams(vmem_limit_bytes=40 * 1024 * 1024),
        cost_estimate=pl.CostEstimate(flops=int(flops), bytes_accessed=0, transcendentals=0),
    )


def chunk_bounds(width, hops):
    tiles = width // 128
    step = 0.25 / max(1, hops - 1)
    return [0] + [int(tiles * (0.2 + step * k)) * 128 for k in range(hops)] + [(tiles - max(1, tiles * 2 // 27)) * 128, width]


def on_device(blocks, feats, layer_input, hidden_grad, hidden_act, output_grad):
    rows, narrow = layer_input.shape
    wide = hidden_grad.shape[1]
    share = rows // TOK
    share_rows = -(-share // 8) * 8
    chips = blocks // 2
    hops = [1 << k for k in range(feats.bit_length() - 1)]
    cuts = chunk_bounds(wide, len(hops))
    me = lax.axis_index("ex")
    chip = me // 2

    def send(value, target):
        pairs = [(e * feats + z, target(e, z)) for e in range(blocks) for z in range(feats)]
        return lax.ppermute(value, ("ex", "feat"), [(i, e * feats + z) for i, (e, z) in pairs])

    def across(value, d):
        return send(value, lambda e, z: (e ^ (2 * d + 1 - parity(z, feats)), z))

    def sibling(value):
        return send(value, lambda e, z: (e ^ 1, z))

    def add_feat(value, sent, hop):
        return value + send(sent, lambda e, z: (e ^ 1, z ^ hop)).astype(F32)

    def struct(r, c, dtype=F32):
        return jax.ShapeDtypeStruct((r, c), dtype)

    lower = [(chip & (1 << (d.bit_length() - 1))) == 0 for d in range(1, chips)]
    picked = [jnp.where(low, layer_input, output_grad) for low in lower]
    picked, layer_input, output_grad, hidden_grad, hidden_act = lax.optimization_barrier(
        (picked, layer_input, output_grad, hidden_grad, hidden_act)
    )
    got_narrow = [across(v, d) for d, v in enumerate(picked, start=1)]
    sib_in, sib_og = sibling(layer_input), sibling(output_grad)

    size = packed_rows(rows, rows)
    local_rows = 2 * size + diagonal_rows(rows)
    local, sent = call(functools.partial(narrow_local_kernel, feats), 4, (struct(local_rows, 128), struct(local_rows, 128, BF16)), 0)(
        layer_input, output_grad, sib_in, sib_og
    )
    sent, hidden_grad, hidden_act = lax.optimization_barrier((sent, hidden_grad, hidden_act))
    sends = [jnp.where(low, hidden_grad, hidden_act) for low in lower]
    got_wide = [
        [across(v[:, b:e], d) for b, e in zip(cuts[:-2], cuts[1:-1])] for d, v in enumerate(sends, start=1)
    ]
    sib_hg, sib_ha = sibling(hidden_grad), sibling(hidden_act)

    for hop in hops:
        local = add_feat(local, sent, hop)
        sent = local.astype(BF16)
        if hop == 1:
            sent, sib_hg, sib_ha = lax.optimization_barrier((sent, sib_hg, sib_ha))
            got_narrow, _ = lax.optimization_barrier((got_narrow, local))
    totals, accs, sents, mines = [], [], [], []
    for d, low in enumerate(lower):
        mine_narrow = jnp.concatenate([jnp.where(low, output_grad, layer_input), jnp.where(low, sib_og, sib_in)], axis=0)
        mine = jnp.concatenate([jnp.where(low, hidden_act, hidden_grad), jnp.where(low, sib_ha, sib_hg)], axis=0)
        total, sent, acc = call(
            functools.partial(first_cross_kernel, feats), 4, (struct(2 * size, 128), struct(2 * size, 128, BF16), struct(2 * rows, rows)), 0
        )(mine_narrow, got_narrow[d], mine[:, : cuts[1]], got_wide[d][0])
        totals.append(total), sents.append(sent), accs.append(acc), mines.append(mine)
    for step, hop in enumerate(hops):
        if step:
            for d in range(chips - 1):
                accs[d] = call(next_cross_kernel, 3, struct(2 * rows, rows), PIECE)(
                    mines[d][:, cuts[step] : cuts[step + 1]], got_wide[d][step], accs[d]
                )
            if step == len(hops) - 1:
                totals, accs, local = lax.optimization_barrier((totals, accs, local))
            else:
                totals, accs = lax.optimization_barrier((totals, accs))
            sents = [t.astype(BF16) for t in totals]
        totals = [add_feat(t, s, hop) for t, s in zip(totals, sents)]

    packed = call(functools.partial(wide_local_kernel, feats), 5, struct(share_rows, 128), LOCAL)(hidden_grad, hidden_act, sib_hg, sib_ha, local)
    last_sends, packed = lax.optimization_barrier(([v[:, cuts[-2] :] for v in sends], packed))
    for d, v in enumerate(last_sends, start=1):
        got_wide[d - 1].append(across(v, d))
    parts = [packed]
    for d in range(chips - 1):
        accs[d] = call(next_cross_kernel, 3, struct(2 * rows, rows), LAST)(
            mines[d][:, cuts[-3] : cuts[-2]], got_wide[d][-2], accs[d]
        )
        start = packed if d == 0 else jnp.zeros((share_rows, 128), F32)
        done = call(functools.partial(wide_last_kernel, feats), 5, struct(share_rows, 128), LAST)(
            mines[d][:, cuts[-2] :], got_wide[d][-1], accs[d], totals[d], start
        )
        if d == 0:
            parts = [done]
        else:
            parts.append(done[:, 2 * SLOT :])
    mine = parts[0] if len(parts) == 1 else jnp.concatenate(parts, axis=1)
    for hop in hops:
        mine = add_feat(mine, mine, hop)
    others = [across(mine, d) for d in range(1, chips)]
    return call(
        functools.partial(final_kernel, blocks, feats, share), 1 + blocks // 2, struct(share, share * blocks // feats), 0, [pltpu.VMEM((SLOT * blocks, 128), F32)]
    )(mine, sibling(mine), *others)


def solution(mesh):
    spec = P(("groups", "ex"), "feat")
    return jax.shard_map(
        functools.partial(on_device, mesh.shape["ex"], mesh.shape["feat"]),
        mesh=mesh,
        in_specs=(spec, spec, spec, spec),
        out_specs=spec,
        check_vma=False,
    )
```
